32 devices in a mesh: rows: 4 (over y, core), cent: 8 (over z, x).
Axes of the slice: x: 2, y: 2, z: 4, core: 2. Of those that a mesh axis runs over, the one named last changes fastest.
Arguments:
- embeddings: bfloat16 [256, 1024], P(('rows', 'cent')), may hold values from -36 to 36
- centroids: bfloat16 [32768, 1024], P(('rows', 'cent')), may hold values from -1 to 1
Outputs:
- row_lse: float32 [256], P(('rows', 'cent'))
- weighted_sums: bfloat16 [32768, 1024], P(('rows', 'cent'))
- counts: float32 [32768], P(('rows', 'cent'))
The draws below stay inside these ranges and needn't reach their ends.
All inputs are finite; a program needn't handle non-finite values.
Results may differ from the reference program's by a relative error of at most 0.0075.
Values may be sent and summed in bfloat16 or wider, within the bound.
A program may use at most 64 MiB of HBM per device.

```python
import math
import jax
import jax.numpy as jnp
from jax import lax

D = 1024
ANCHORS = 8
K = 32768
N = 256
N_ROWS = 4
N_CENT = 8


support_width = 8


def anchor_rows(key):
    signs = jnp.where(jax.random.bernoulli(key, 0.5, (ANCHORS, D)), 1.0, -1.0)
    owner = jnp.arange(D) // support_width
    support = owner[None, :] == jnp.arange(ANCHORS)[:, None]
    return jnp.where(support, signs / math.sqrt(support_width), 0.0).astype(jnp.float32)


def draw_centroids(key, part):
    table = anchor_rows(key)
    key = jax.random.fold_in(key, 11)
    base = jax.random.truncated_normal(key, -6.0, 6.0, (K, D), jnp.float32) / math.sqrt(D)
    rising = jnp.exp(math.log(1.05) * jnp.arange(K, dtype=jnp.float32) / K)
    base = jnp.clip(base * rising[:, None], -1.0, 1.0)
    spots = jnp.arange(ANCHORS) * (K // ANCHORS)
    base = base.at[spots].set(table)
    return base.astype(jnp.bfloat16)


def draw_embeddings(key, part):
    key = jax.random.fold_in(key, 12)
    first = jax.random.fold_in(key, 0)
    values = jax.random.truncated_normal(first, -6.0, 6.0, (N, D), jnp.float32)
    return values.astype(jnp.bfloat16)


def setup_inputs(seed: int = 0) -> dict:
    seeds = jax.random.split(jax.random.key(seed), 3)
    embeddings = draw_embeddings(jax.random.fold_in(seeds[2], 71), 0)
    centroids = draw_centroids(jax.random.fold_in(seeds[2], 71), 0)
    return dict(embeddings=embeddings, centroids=centroids)


inverse_temp = 3.0


def reference(embeddings, centroids):
    blocks = centroids.reshape(N_ROWS * N_CENT, -1, D)

    def block_scores(block):
        return inverse_temp * lax.dot_general(embeddings, block, (((1,), (1,)), ((), ())), preferred_element_type=jnp.float32)

    def stats(carry, block):
        scores = block_scores(block)
        running_max, running_total = carry
        newest = jnp.maximum(running_max, jnp.max(scores, axis=1))
        total = running_total * jnp.exp(running_max - newest) + jnp.sum(jnp.exp(scores - newest[:, None]), axis=1)
        return (newest, total), None

    start = (jnp.full((N,), -1.0e30, jnp.float32), jnp.zeros((N,), jnp.float32))
    (largest, total), unused = lax.scan(stats, start, blocks)
    row_lse = largest + jnp.log(total)

    def weigh(block):
        resp = jnp.exp(block_scores(block) - row_lse[:, None]).astype(jnp.bfloat16)
        counts = jnp.sum(resp.astype(jnp.float32), axis=0)
        sums = lax.dot_general(resp, embeddings, (((0,), (0,)), ((), ())), preferred_element_type=jnp.float32)
        return counts, sums.astype(jnp.bfloat16)

    counts, sums = lax.map(weigh, blocks)
    return row_lse, sums.reshape(K, D), counts.reshape(K)
```

```python
import functools

import jax
import jax.numpy as jnp
from jax import lax
from jax.experimental import pallas as pl
from jax.experimental.pallas import tpu as pltpu
from jax.sharding import PartitionSpec as P

inverse_temp = 3.0
MESH = pl.DeviceIdType.MESH
NT = (((1,), (1,)), ((), ()))
NN = (((1,), (0,)), ((), ()))


def kernel(
    sizes, emb, cen, lse_out, counts_out, sums_out,
    cen_v, slots, gathered, shifted, resp, sums_v, stats,
    cen_sem, z_send, z_recv, p_send, p_recv, c_send, c_recv, s_send, s_recv, out_sem,
):
    Y, X, Z = sizes
    devices = 2 * Y * X * Z
    cents = X * Z
    n, depth = gathered.shape
    half = depth // 2
    k = cen.shape[0]
    r = lax.axis_index("rows")
    c = lax.axis_index("cent")
    y, core = r // 2, r % 2
    z, x = c // X, c % X

    def place(y_, core_, z_, x_):
        return (y_ * 2 + core_, z_ * X + x_)

    load = pltpu.make_async_copy(cen, cen_v, cen_sem)
    load.start()

    z_peers = [place(y, core, (z + i) % Z, x) for i in range(1, Z)]
    plane = [(i, j) for i in range(Y) for j in range(X) if (i, j) != (0, 0)]
    p_peers = [place((y + i) % Y, core, z, (x + j) % X) for i, j in plane]
    twin = place(y, 1 - core, z, x)

    barrier = pltpu.get_barrier_semaphore()
    for peer in z_peers + p_peers + [twin]:
        pl.semaphore_signal(barrier, inc=1, device_id=peer, device_id_type=MESH)

    def column(core_, y_, x_):
        return ((core_ * Y + y_) * X + x_) * Z

    base = column(core, y, x)
    mine = base + z
    own = emb[...].astype(jnp.float32)
    own = jnp.concatenate([own[:, :half], own[:, half:]], axis=0)
    slots[mine] = own.astype(jnp.bfloat16)
    pl.semaphore_wait(barrier, len(z_peers) + len(p_peers) + 1)

    def send(first, count, send_sem, recv_sem, peer):
        ref = slots.at[pl.ds(first, count)]
        return pltpu.make_async_remote_copy(
            src_ref=ref, dst_ref=ref, send_sem=send_sem, recv_sem=recv_sem,
            device_id=peer, device_id_type=MESH,
        )

    z_copies = [
        send(mine, 1, z_send.at[i], z_recv.at[i], peer) for i, peer in enumerate(z_peers)
    ]
    for copy in z_copies:
        copy.start()
    for copy in z_copies:
        copy.wait_recv()
    p_copies = [
        send(base, Z, p_send.at[i], p_recv.at[i], peer) for i, peer in enumerate(p_peers)
    ]
    for copy in p_copies:
        copy.start()
    c_copies = [send(base, Z, c_send.at[0], c_recv.at[0], twin)]
    c_copies[0].start()
    for i, (copy, (dy, dx)) in enumerate(zip(p_copies, plane)):
        copy.wait_recv()
        first = column(core, (y - dy + Y) % Y, (x - dx + X) % X)
        c_copies.append(send(first, Z, c_send.at[i + 1], c_recv.at[i + 1], twin))
        c_copies[-1].start()
    for copy in c_copies:
        copy.wait_recv()
    for copy in z_copies + p_copies + c_copies:
        copy.wait_send()

    step = min(8, devices)

    @pl.loop(0, devices // step)
    def _(i):
        part = slots[pl.ds(i * step, step)].astype(jnp.float32)
        rows = pl.ds(pl.multiple_of(i * step * 8, step * 8), step * 8)
        gathered[rows, :half] = part[:, :8].reshape(step * 8, half).astype(jnp.bfloat16)
        gathered[rows, half:] = part[:, 8:].reshape(step * 8, half).astype(jnp.bfloat16)

    load.wait()

    tile = 256
    wide = min(n, 256)

    @pl.loop(0, n // wide)
    def _(j):
        lanes = pl.ds(pl.multiple_of(j * wide, wide), wide)
        top = jnp.full((8, wide), -jnp.inf, jnp.float32)
        for t in range(k // tile):
            rows = pl.ds(t * tile, tile)
            part = inverse_temp * lax.dot_general(
                cen_v[rows, :], gathered[lanes, :], NT, preferred_element_type=jnp.float32
            )
            shifted[rows, lanes] = part
            top = jnp.maximum(top, jnp.max(part.reshape(tile // 8, 8, wide), axis=0))
        top = jnp.max(top, axis=0, keepdims=True)
        total = jnp.zeros((8, wide), jnp.float32)
        for t in range(k // tile):
            rows = pl.ds(t * tile, tile)
            part = jnp.exp(shifted[rows, lanes] - top)
            shifted[rows, lanes] = part
            total = total + jnp.sum(part.reshape(tile // 8, 8, wide), axis=0)
        stats[r * cents + c, 0:1, lanes] = top
        stats[r * cents + c, 1:2, lanes] = jnp.sum(total, axis=0, keepdims=True)

    me = r * cents + c

    def stat_copy(i):
        peer = (me + i) % devices
        return pltpu.make_async_remote_copy(
            src_ref=stats.at[me], dst_ref=stats.at[me], send_sem=s_send, recv_sem=s_recv,
            device_id=(peer // cents, peer % cents), device_id_type=MESH,
        )

    @pl.loop(1, devices)
    def _(i):
        stat_copy(i).start()

    others = stats.at[pl.ds(0, devices - 1)]
    pltpu.make_async_copy(others, others, s_recv).wait()

    @pl.loop(0, n // wide)
    def _(j):
        lanes = pl.ds(pl.multiple_of(j * wide, wide), wide)
        tops = stats[:, 0:1, lanes]
        top = jnp.max(tops, axis=0)
        total = jnp.sum(stats[:, 1:2, lanes] * jnp.exp(tops - top[None]), axis=0)
        lse = top + jnp.log(total)
        lse_out[:, lanes] = lse
        factor = jnp.exp(stats[me, 0:1, lanes] - lse)
        for t in range(k // tile):
            rows = pl.ds(t * tile, tile)
            resp[rows, lanes] = (shifted[rows, lanes] * factor).astype(jnp.bfloat16)

    counts_out[...] = lax.dot_general(
        jnp.ones((8, n), jnp.bfloat16), resp[...], NT, preferred_element_type=jnp.float32
    )[0:1]

    outs = []
    for t in range(k // tile):
        rows = pl.ds(t * tile, tile)
        sums_v[rows, :] = lax.dot_general(
            resp[rows, :], gathered[...], NN, preferred_element_type=jnp.float32
        ).astype(jnp.bfloat16)
        outs.append(pltpu.make_async_copy(sums_v.at[rows], sums_out.at[rows], out_sem.at[t]))
        outs[-1].start()
    pltpu.make_async_copy(others, others, s_send).wait()
    for copy in outs:
        copy.wait()


def on_device(sizes, embeddings, centroids):
    Y, X, Z = sizes
    devices = 2 * Y * X * Z
    local, depth = embeddings.shape
    k = centroids.shape[0]
    n = local * devices
    dma = pltpu.SemaphoreType.DMA
    planes = Y * X - 1
    vmem = pl.BlockSpec(memory_space=pltpu.VMEM)
    lse, counts, sums = pl.pallas_call(
        functools.partial(kernel, sizes),
        out_shape=(
            jax.ShapeDtypeStruct((1, n), jnp.float32),
            jax.ShapeDtypeStruct((1, k), jnp.float32),
            jax.ShapeDtypeStruct((k, depth), jnp.bfloat16),
        ),
        in_specs=[vmem, pl.BlockSpec(memory_space=pl.ANY)],
        out_specs=(vmem, vmem, pl.BlockSpec(memory_space=pl.ANY)),
        scratch_shapes=[
            pltpu.VMEM((k, depth), jnp.bfloat16),
            pltpu.VMEM((devices, 2 * local, depth // 2), jnp.bfloat16),
            pltpu.VMEM((n, depth), jnp.bfloat16),
            pltpu.VMEM((k, n), jnp.float32),
            pltpu.VMEM((k, n), jnp.bfloat16),
            pltpu.VMEM((k, depth), jnp.bfloat16),
            pltpu.VMEM((devices, 2, n), jnp.float32),
            dma,
            dma((Z - 1,)), dma((Z - 1,)),
            dma((planes,)), dma((planes,)),
            dma((planes + 1,)), dma((planes + 1,)),
            dma, dma,
            dma((k // 256,)),
        ],
        compiler_params=pltpu.CompilerParams(
            collective_id=0, has_side_effects=True, vmem_limit_bytes=48 * 2**20
        ),
    )(embeddings, centroids)
    y, core = lax.axis_index("rows") // 2, lax.axis_index("rows") % 2
    z, x = lax.axis_index("cent") // X, lax.axis_index("cent") % X
    slot = ((core * Y + y) * X + x) * Z + z
    own_lse = lax.dynamic_slice_in_dim(lse.reshape(n), slot * local, local, 0)
    return own_lse, sums, counts.reshape(k)


def solution(mesh):
    rows, cents = mesh.shape["rows"], mesh.shape["cent"]
    Y = rows // 2
    X = Y if cents % Y == 0 else 1
    return jax.shard_map(
        functools.partial(on_device, (Y, X, cents // X)),
        mesh=mesh,
        in_specs=(P(("rows", "cent"), None), P(("rows", "cent"), None)),
        out_specs=(P(("rows", "cent")), P(("rows", "cent"), None), P(("rows", "cent"))),
        check_vma=False,
    )
```

```python
import functools

import jax
import jax.numpy as jnp
from jax import lax
from jax.experimental import pallas as pl
from jax.experimental.pallas import tpu as pltpu
from jax.sharding import PartitionSpec as P

inverse_temp = 3.0
MESH = pl.DeviceIdType.MESH
NT = (((1,), (1,)), ((), ()))
SUMS_TILE = 256
NN = (((1,), (0,)), ((), ()))


def flipped(index, size, mask):
    if size & (size - 1):
        return (index + mask) % size
    bit = 1
    while bit < size:
        if mask & bit:
            index = index + bit - 2 * bit * ((index // bit) % 2)
        bit *= 2
    return index


def sender(index, size, mask):
    if size & (size - 1):
        return (index + size - mask) % size
    return flipped(index, size, mask)


def spread_kernel(
    sizes, emb, cen, lse_out, resp, gathered,
    cen_v, slots, shifted, stats,
    own_sem, cen_sem, b_send, b_recv, c_send, c_recv, s_send, s_recv,
):
    Y, X, Z = sizes
    devices = 2 * Y * X * Z
    cents = X * Z
    n = gathered.shape[0]
    local = emb.shape[0]
    k = cen.shape[0]
    r = lax.axis_index("rows")
    c = lax.axis_index("cent")
    y, core = r // 2, r % 2
    z, x = c // X, c % X

    def place(y_, core_, z_, x_):
        return (y_ * 2 + core_, z_ * X + x_)

    def slot_of(y_, core_, z_, x_):
        return ((core_ * Y + y_) * X + x_) * Z + z_

    plane = [(i, j) for i in range(Y) for j in range(X)]
    z_peers = [place(y, core, flipped(z, Z, i), x) for i in range(Z)]
    p_peers = [place(flipped(y, Y, i), core, z, flipped(x, X, j)) for i, j in plane]
    twin = place(y, 1 - core, z, x)

    barrier = pltpu.get_barrier_semaphore()
    for peer in z_peers[1:] + p_peers[1:] + [twin]:
        pl.semaphore_signal(barrier, inc=1, device_id=peer, device_id_type=MESH)
    mine = slot_of(y, core, z, x)
    load_own = pltpu.make_async_copy(emb, slots.at[mine], own_sem)
    load_own.start()
    load = pltpu.make_async_copy(cen, cen_v, cen_sem)
    load.start()
    pl.semaphore_wait(barrier, len(z_peers) + len(p_peers) - 1)

    def send(src, slot, sems, peer):
        return pltpu.make_async_remote_copy(
            src_ref=src, dst_ref=slots.at[slot], send_sem=sems[0], recv_sem=sems[1],
            device_id=peer, device_id_type=MESH,
        )

    def link_sems(i, p):
        return b_send.at[i, p], b_recv.at[i, p]

    def block_slot(i, p):
        dy, dx = plane[p]
        return slot_of(sender(y, Y, dy), core, sender(z, Z, i), sender(x, X, dx))

    started = []
    def start(copy):
        copy.start()
        started.append(copy)
        return copy

    def to_plane(i, src):
        return [
            start(send(src, block_slot(i, 0), link_sems(i, p), p_peers[p]))
            for p in range(1, len(plane))
        ]

    def to_twin(i, p, src):
        return start(send(src, block_slot(i, p), (c_send.at[i, p], c_recv.at[i, p]), twin))

    arrivals = {}
    for i in range(Z - 1, 0, -1):
        arrivals[i, 0] = start(send(emb, mine, link_sems(i, 0), z_peers[i]))
    for p, copy in enumerate(to_plane(0, emb)):
        arrivals[0, p + 1] = copy
    over = [to_twin(0, 0, emb)]
    for i in range(1, Z):
        arrivals[i, 0].wait_recv()
        src = slots.at[block_slot(i, 0)]
        for p, copy in enumerate(to_plane(i, src)):
            arrivals[i, p + 1] = copy
        over.append(to_twin(i, 0, src))
    for i in range(Z):
        for p in range(1, len(plane)):
            arrivals[i, p].wait_recv()
            over.append(to_twin(i, p, slots.at[block_slot(i, p)]))
    load_own.wait()

    step = min(8, devices // 2)

    def lay_out(first):
        @pl.loop(0, devices // 2 // step)
        def _(i):
            part = slots[pl.ds(first + i * step, step)].astype(jnp.float32)
            rows = pl.ds(pl.multiple_of((first + i * step) * local, step * local), step * local)
            gathered[rows, :] = part.reshape(step * local, part.shape[2]).astype(jnp.bfloat16)

    lay_out(core * (devices // 2))
    load.wait()
    for copy in over:
        copy.wait_recv()
    lay_out((1 - core) * (devices // 2))
    tile = 256
    wide = min(n, 256)
    me = r * cents + c

    @pl.loop(0, n // wide)
    def _(j):
        lanes = pl.ds(pl.multiple_of(j * wide, wide), wide)
        top = jnp.full((8, wide), -jnp.inf, jnp.float32)
        for t in range(k // tile):
            rows = pl.ds(t * tile, tile)
            part = inverse_temp * lax.dot_general(
                cen_v[rows, :], gathered[lanes, :], NT, preferred_element_type=jnp.float32
            )
            shifted[rows, lanes] = part
            top = jnp.maximum(top, jnp.max(part.reshape(tile // 8, 8, wide), axis=0))
        top = jnp.max(top, axis=0, keepdims=True)
        total = jnp.zeros((8, wide), jnp.float32)
        for t in range(k // tile):
            rows = pl.ds(t * tile, tile)
            part = jnp.exp(shifted[rows, lanes] - top)
            shifted[rows, lanes] = part
            total = total + jnp.sum(part.reshape(tile // 8, 8, wide), axis=0)
        stats[me, 0:1, lanes] = top
        stats[me, 1:2, lanes] = jnp.sum(total, axis=0, keepdims=True)

    offsets = [
        (i, j, l, m) for l in range(Z) for i in range(Y) for j in range(X) for m in range(2)
    ]
    for i, j, l, m in reversed(offsets[1:]):
        peer = place(flipped(y, Y, i), (core + m) % 2, flipped(z, Z, l), flipped(x, X, j))
        pltpu.make_async_remote_copy(
            src_ref=stats.at[me], dst_ref=stats.at[me], send_sem=s_send, recv_sem=s_recv,
            device_id=peer, device_id_type=MESH,
        ).start()
    for copy in started:
        copy.wait_send()

    others = stats.at[pl.ds(0, devices - 1)]
    pltpu.make_async_copy(others, others, s_recv).wait()

    @pl.loop(0, n // wide)
    def _(j):
        lanes = pl.ds(pl.multiple_of(j * wide, wide), wide)
        tops = stats[:, 0:1, lanes]
        top = jnp.max(tops, axis=0)
        total = jnp.sum(stats[:, 1:2, lanes] * jnp.exp(tops - top[None]), axis=0)
        lse = top + jnp.log(total)
        lse_out[:, lanes] = lse
        factor = jnp.exp(stats[me, 0:1, lanes] - lse)
        for t in range(k // tile):
            rows = pl.ds(t * tile, tile)
            resp[rows, lanes] = (shifted[rows, lanes] * factor).astype(jnp.bfloat16)

    pltpu.make_async_copy(others, others, s_send).wait()


def sums_kernel(
    sizes, lse, resp, gathered, lse_out, counts_out, sums_out,
    lse_v, counts_v, sums_v, lse_sem, counts_sem, out_sem,
):
    Y, X, Z = sizes
    n = gathered.shape[0]
    k = resp.shape[0]
    local = lse_out.shape[1]
    r = lax.axis_index("rows")
    c = lax.axis_index("cent")
    slot = (((r % 2) * Y + r // 2) * X + c % X) * Z + c // X

    outs = []
    for t in range(k // SUMS_TILE):
        rows = pl.ds(t * SUMS_TILE, SUMS_TILE)
        sums_v[rows, :] = lax.dot_general(
            resp[rows, :], gathered[...], NN, preferred_element_type=jnp.float32
        ).astype(jnp.bfloat16)
        outs.append(pltpu.make_async_copy(sums_v.at[rows], sums_out.at[rows], out_sem.at[t]))
        outs[-1].start()
        if t == 0:
            rolled = pltpu.roll(jnp.broadcast_to(lse[...], (8, n)), n - slot * local, 1)
            lse_v[...] = rolled[0:1, :local]
            outs.append(pltpu.make_async_copy(lse_v, lse_out, lse_sem))
            outs[-1].start()
            counts_v[...] = lax.dot_general(
                jnp.ones((8, n), jnp.bfloat16), resp[...], NT,
                preferred_element_type=jnp.float32,
            )[0:1]
            outs.append(pltpu.make_async_copy(counts_v, counts_out, counts_sem))
            outs[-1].start()
    for copy in outs:
        copy.wait()


def on_device(sizes, embeddings, centroids):
    Y, X, Z = sizes
    devices = 2 * Y * X * Z
    local, depth = embeddings.shape
    k = centroids.shape[0]
    n = local * devices
    dma = pltpu.SemaphoreType.DMA
    vmem = pl.BlockSpec(memory_space=pltpu.VMEM)
    hbm = pl.BlockSpec(memory_space=pltpu.HBM)
    embeddings = pltpu.with_memory_space_constraint(embeddings, pltpu.HBM)
    centroids = pltpu.with_memory_space_constraint(centroids, pltpu.HBM)
    lse, resp, gathered = pl.pallas_call(
        functools.partial(spread_kernel, sizes),
        out_shape=(
            jax.ShapeDtypeStruct((1, n), jnp.float32),
            jax.ShapeDtypeStruct((k, n), jnp.bfloat16),
            jax.ShapeDtypeStruct((n, depth), jnp.bfloat16),
        ),
        in_specs=[hbm, hbm],
        out_specs=(vmem, vmem, vmem),
        scratch_shapes=[
            pltpu.VMEM((k, depth), jnp.bfloat16),
            pltpu.VMEM((devices, local, depth), jnp.bfloat16),
            pltpu.VMEM((k, n), jnp.float32),
            pltpu.VMEM((devices, 2, n), jnp.float32),
            dma, dma,
            dma((Z, Y * X)), dma((Z, Y * X)),
            dma((Z, Y * X)), dma((Z, Y * X)),
            dma, dma,
        ],
        compiler_params=pltpu.CompilerParams(
            collective_id=0, has_side_effects=True, vmem_limit_bytes=32 * 2**20
        ),
    )(embeddings, centroids)
    own_lse, counts, sums = pl.pallas_call(
        functools.partial(sums_kernel, sizes),
        out_shape=(
            jax.ShapeDtypeStruct((1, local), jnp.float32),
            jax.ShapeDtypeStruct((1, k), jnp.float32),
            jax.ShapeDtypeStruct((k, depth), jnp.bfloat16),
        ),
        in_specs=[vmem, vmem, vmem],
        out_specs=(hbm, hbm, hbm),
        scratch_shapes=[
            pltpu.VMEM((1, local), jnp.float32),
            pltpu.VMEM((1, k), jnp.float32),
            pltpu.VMEM((k, depth), jnp.bfloat16),
            dma, dma,
            dma((k // SUMS_TILE,)),
        ],
        compiler_params=pltpu.CompilerParams(vmem_limit_bytes=16 * 2**20),
    )(lse, resp, gathered)
    return own_lse.reshape(local), sums, counts.reshape(k)


def solution(mesh):
    rows, cents = mesh.shape["rows"], mesh.shape["cent"]
    Y = rows // 2
    X = Y if cents % Y == 0 else 1
    return jax.shard_map(
        functools.partial(on_device, (Y, X, cents // X)),
        mesh=mesh,
        in_specs=(P(("rows", "cent"), None), P(("rows", "cent"), None)),
        out_specs=(P(("rows", "cent")), P(("rows", "cent"), None), P(("rows", "cent"))),
        check_vma=False,
    )
```

```python
import functools

import jax
import jax.numpy as jnp
from jax import lax
from jax.experimental import pallas as pl
from jax.experimental.pallas import tpu as pltpu
from jax.sharding import PartitionSpec as P

inverse_temp = 3.0
MESH = pl.DeviceIdType.MESH
NT = (((1,), (1,)), ((), ()))
SUMS_TILE = 256
NN = (((1,), (0,)), ((), ()))


def flipped(index, size, mask):
    if size & (size - 1):
        return (index + mask) % size
    bit = 1
    while bit < size:
        if mask & bit:
            index = index + bit - 2 * bit * ((index // bit) % 2)
        bit *= 2
    return index


def sender(index, size, mask):
    if size & (size - 1):
        return (index + size - mask) % size
    return flipped(index, size, mask)


def spread_kernel(
    sizes, emb, cen, lse_out, resp, gathered,
    cen_v, slots, shifted, tops, stats,
    own_sem, cen_sem, b_send, b_recv, c_send, c_recv, s_send, s_recv,
):
    Y, X, Z = sizes
    devices = 2 * Y * X * Z
    cents = X * Z
    n = gathered.shape[0]
    local = emb.shape[0]
    k = cen.shape[0]
    r = lax.axis_index("rows")
    c = lax.axis_index("cent")
    y, core = r // 2, r % 2
    z, x = c // X, c % X

    def place(y_, core_, z_, x_):
        return (y_ * 2 + core_, z_ * X + x_)

    def slot_of(y_, core_, z_, x_):
        return ((core_ * Y + y_) * X + x_) * Z + z_

    plane = [(i, j) for i in range(Y) for j in range(X)]
    z_peers = [place(y, core, flipped(z, Z, i), x) for i in range(Z)]
    p_peers = [place(flipped(y, Y, i), core, z, flipped(x, X, j)) for i, j in plane]
    twin = place(y, 1 - core, z, x)

    barrier = pltpu.get_barrier_semaphore()
    for peer in z_peers[1:] + p_peers[1:] + [twin]:
        pl.semaphore_signal(barrier, inc=1, device_id=peer, device_id_type=MESH)
    mine = slot_of(y, core, z, x)
    load_own = pltpu.make_async_copy(emb, slots.at[mine], own_sem)
    load_own.start()
    load = pltpu.make_async_copy(cen, cen_v, cen_sem)
    load.start()
    pl.semaphore_wait(barrier, len(z_peers) + len(p_peers) - 1)

    def send(src, slot, sems, peer):
        return pltpu.make_async_remote_copy(
            src_ref=src, dst_ref=slots.at[slot], send_sem=sems[0], recv_sem=sems[1],
            device_id=peer, device_id_type=MESH,
        )

    def link_sems(i, p):
        return b_send.at[i, p], b_recv.at[i, p]

    def block_slot(i, p):
        dy, dx = plane[p]
        return slot_of(sender(y, Y, dy), core, sender(z, Z, i), sender(x, X, dx))

    started = []
    def start(copy):
        copy.start()
        started.append(copy)
        return copy

    def to_plane(i, src):
        return [
            start(send(src, block_slot(i, 0), link_sems(i, p), p_peers[p]))
            for p in range(len(plane) - 1, 0, -1)
        ][::-1]

    def to_twin(i, p, src):
        return start(send(src, block_slot(i, p), (c_send.at[i, p], c_recv.at[i, p]), twin))

    arrivals = {}
    for i in range(Z - 1, 0, -1):
        arrivals[i, 0] = start(send(emb, mine, link_sems(i, 0), z_peers[i]))
    for p, copy in enumerate(to_plane(0, emb)):
        arrivals[0, p + 1] = copy
    over = [to_twin(0, 0, emb)]
    for i in range(1, Z):
        arrivals[i, 0].wait_recv()
        src = slots.at[block_slot(i, 0)]
        for p, copy in enumerate(to_plane(i, src)):
            arrivals[i, p + 1] = copy
        over.append(to_twin(i, 0, src))
    for i in range(Z):
        for p in range(1, len(plane)):
            arrivals[i, p].wait_recv()
            over.append(to_twin(i, p, slots.at[block_slot(i, p)]))
    load_own.wait()

    step = min(8, devices // 2)

    def lay_out(first):
        @pl.loop(0, devices // 2 // step)
        def _(i):
            part = slots[pl.ds(first + i * step, step)].astype(jnp.float32)
            rows = pl.ds(pl.multiple_of((first + i * step) * local, step * local), step * local)
            gathered[rows, :] = part.reshape(step * local, part.shape[2]).astype(jnp.bfloat16)

    lay_out(core * (devices // 2))
    load.wait()
    for copy in over:
        copy.wait_recv()
    lay_out((1 - core) * (devices // 2))
    tile = 256
    wide = min(n, 256)
    me = r * cents + c

    @pl.loop(0, n // wide)
    def _(j):
        lanes = pl.ds(pl.multiple_of(j * wide, wide), wide)
        top = jnp.full((8, wide), -jnp.inf, jnp.float32)
        for t in range(k // tile):
            rows = pl.ds(t * tile, tile)
            part = inverse_temp * lax.dot_general(
                cen_v[rows, :], gathered[lanes, :], NT, preferred_element_type=jnp.float32
            )
            shifted[rows, lanes] = part
            top = jnp.maximum(top, jnp.max(part.reshape(tile // 8, 8, wide), axis=0))
        top = jnp.max(top, axis=0, keepdims=True)
        total = jnp.zeros((8, wide), jnp.float32)
        for t in range(k // tile):
            rows = pl.ds(t * tile, tile)
            part = jnp.exp(shifted[rows, lanes] - top)
            shifted[rows, lanes] = part
            total = total + jnp.sum(part.reshape(tile // 8, 8, wide), axis=0)
        tops[:, lanes] = top
        stats[me, :, lanes] = top + jnp.log(jnp.sum(total, axis=0, keepdims=True))

    offsets = [
        (i, j, l, m) for l in range(Z) for i in range(Y) for j in range(X) for m in range(2)
    ]
    for i, j, l, m in reversed(offsets[1:]):
        peer = place(flipped(y, Y, i), (core + m) % 2, flipped(z, Z, l), flipped(x, X, j))
        pltpu.make_async_remote_copy(
            src_ref=stats.at[me], dst_ref=stats.at[me], send_sem=s_send, recv_sem=s_recv,
            device_id=peer, device_id_type=MESH,
        ).start()
    for copy in started:
        copy.wait_send()

    others = stats.at[pl.ds(0, devices - 1)]
    pltpu.make_async_copy(others, others, s_recv).wait()

    @pl.loop(0, n // wide)
    def _(j):
        lanes = pl.ds(pl.multiple_of(j * wide, wide), wide)
        part_lse = stats[:, :, lanes]
        top = jnp.max(part_lse, axis=0)
        lse = top + jnp.log(jnp.sum(jnp.exp(part_lse - top[None]), axis=0))
        lse_out[:, lanes] = lse
        factor = jnp.exp(tops[:, lanes] - lse)
        for t in range(k // tile):
            rows = pl.ds(t * tile, tile)
            resp[rows, lanes] = (shifted[rows, lanes] * factor).astype(jnp.bfloat16)

    pltpu.make_async_copy(others, others, s_send).wait()


def sums_kernel(
    sizes, lse, resp, gathered, lse_out, counts_out, sums_out,
    lse_v, counts_v, sums_v, lse_sem, counts_sem, out_sem,
):
    Y, X, Z = sizes
    n = gathered.shape[0]
    k = resp.shape[0]
    local = lse_out.shape[1]
    r = lax.axis_index("rows")
    c = lax.axis_index("cent")
    slot = (((r % 2) * Y + r // 2) * X + c % X) * Z + c // X

    outs = []
    for t in range(k // SUMS_TILE):
        rows = pl.ds(t * SUMS_TILE, SUMS_TILE)
        sums_v[rows, :] = lax.dot_general(
            resp[rows, :], gathered[...], NN, preferred_element_type=jnp.float32
        ).astype(jnp.bfloat16)
        outs.append(pltpu.make_async_copy(sums_v.at[rows], sums_out.at[rows], out_sem.at[t]))
        outs[-1].start()
        if t == 1:
            rolled = pltpu.roll(jnp.broadcast_to(lse[...], (8, n)), n - slot * local, 1)
            lse_v[...] = rolled[0:1, :local]
            outs.append(pltpu.make_async_copy(lse_v, lse_out, lse_sem))
            outs[-1].start()
            counts_v[...] = lax.dot_general(
                jnp.ones((8, n), jnp.bfloat16), resp[...], NT,
                preferred_element_type=jnp.float32,
            )[0:1]
            outs.append(pltpu.make_async_copy(counts_v, counts_out, counts_sem))
            outs[-1].start()
    for copy in outs:
        copy.wait()


def on_device(sizes, embeddings, centroids):
    Y, X, Z = sizes
    devices = 2 * Y * X * Z
    local, depth = embeddings.shape
    k = centroids.shape[0]
    n = local * devices
    dma = pltpu.SemaphoreType.DMA
    vmem = pl.BlockSpec(memory_space=pltpu.VMEM)
    hbm = pl.BlockSpec(memory_space=pltpu.HBM)
    embeddings = pltpu.with_memory_space_constraint(embeddings, pltpu.HBM)
    centroids = pltpu.with_memory_space_constraint(centroids, pltpu.HBM)
    lse, resp, gathered = pl.pallas_call(
        functools.partial(spread_kernel, sizes),
        out_shape=(
            jax.ShapeDtypeStruct((1, n), jnp.float32),
            jax.ShapeDtypeStruct((k, n), jnp.bfloat16),
            jax.ShapeDtypeStruct((n, depth), jnp.bfloat16),
        ),
        in_specs=[hbm, hbm],
        out_specs=(vmem, vmem, vmem),
        scratch_shapes=[
            pltpu.VMEM((k, depth), jnp.bfloat16),
            pltpu.VMEM((devices, local, depth), jnp.bfloat16),
            pltpu.VMEM((k, n), jnp.float32),
            pltpu.VMEM((1, n), jnp.float32),
            pltpu.VMEM((devices, 1, n), jnp.float32),
            dma, dma,
            dma((Z, Y * X)), dma((Z, Y * X)),
            dma((Z, Y * X)), dma((Z, Y * X)),
            dma, dma,
        ],
        compiler_params=pltpu.CompilerParams(
            collective_id=0, has_side_effects=True, vmem_limit_bytes=32 * 2**20
        ),
    )(embeddings, centroids)
    own_lse, counts, sums = pl.pallas_call(
        functools.partial(sums_kernel, sizes),
        out_shape=(
            jax.ShapeDtypeStruct((1, local), jnp.float32),
            jax.ShapeDtypeStruct((1, k), jnp.float32),
            jax.ShapeDtypeStruct((k, depth), jnp.bfloat16),
        ),
        in_specs=[vmem, vmem, vmem],
        out_specs=(hbm, hbm, hbm),
        scratch_shapes=[
            pltpu.VMEM((1, local), jnp.float32),
            pltpu.VMEM((1, k), jnp.float32),
            pltpu.VMEM((k, depth), jnp.bfloat16),
            dma, dma,
            dma((k // SUMS_TILE,)),
        ],
        compiler_params=pltpu.CompilerParams(vmem_limit_bytes=16 * 2**20),
    )(lse, resp, gathered)
    return own_lse.reshape(local), sums, counts.reshape(k)


def solution(mesh):
    rows, cents = mesh.shape["rows"], mesh.shape["cent"]
    Y = rows // 2
    X = Y if cents % Y == 0 else 1
    return jax.shard_map(
        functools.partial(on_device, (Y, X, cents // X)),
        mesh=mesh,
        in_specs=(P(("rows", "cent"), None), P(("rows", "cent"), None)),
        out_specs=(P(("rows", "cent")), P(("rows", "cent"), None), P(("rows", "cent"))),
        check_vma=False,
    )
```

```python
import functools

import jax
import jax.numpy as jnp
from jax import lax
from jax.experimental import pallas as pl
from jax.experimental.pallas import tpu as pltpu
from jax.sharding import PartitionSpec as P

inverse_temp = 3.0
MESH = pl.DeviceIdType.MESH
NT = (((1,), (1,)), ((), ()))
SUMS_TILE = 256
NN = (((1,), (0,)), ((), ()))


def flipped(index, size, mask):
    if size & (size - 1):
        return (index + mask) % size
    bit = 1
    while bit < size:
        if mask & bit:
            index = index + bit - 2 * bit * ((index // bit) % 2)
        bit *= 2
    return index


def sender(index, size, mask):
    if size & (size - 1):
        return (index + size - mask) % size
    return flipped(index, size, mask)


def spread_kernel(
    sizes, emb, cen, lse_out, resp, gathered,
    cen_v, slots, shifted, tops, stats,
    own_sem, cen_sem, b_send, b_recv, c_send, c_recv, s_send, s_recv,
):
    Y, X, Z = sizes
    devices = 2 * Y * X * Z
    cents = X * Z
    n = gathered.shape[0]
    local = emb.shape[0]
    k = cen.shape[0]
    r = lax.axis_index("rows")
    c = lax.axis_index("cent")
    y, core = r // 2, r % 2
    z, x = c // X, c % X

    def place(y_, core_, z_, x_):
        return (y_ * 2 + core_, z_ * X + x_)

    def slot_of(y_, core_, z_, x_):
        return ((core_ * Y + y_) * X + x_) * Z + z_

    plane = [(i, j) for i in range(Y) for j in range(X)]
    z_peers = [place(y, core, flipped(z, Z, i), x) for i in range(Z)]
    p_peers = [place(flipped(y, Y, i), core, z, flipped(x, X, j)) for i, j in plane]
    twin = place(y, 1 - core, z, x)

    barrier = pltpu.get_barrier_semaphore()
    for peer in z_peers[1:] + p_peers[1:] + [twin]:
        pl.semaphore_signal(barrier, inc=1, device_id=peer, device_id_type=MESH)
    mine = slot_of(y, core, z, x)
    load_own = pltpu.make_async_copy(emb, slots.at[mine], own_sem)
    load_own.start()
    load = pltpu.make_async_copy(cen, cen_v, cen_sem)
    pl.semaphore_wait(barrier, len(z_peers) + len(p_peers) - 1)

    def send(src, slot, sems, peer):
        return pltpu.make_async_remote_copy(
            src_ref=src, dst_ref=slots.at[slot], send_sem=sems[0], recv_sem=sems[1],
            device_id=peer, device_id_type=MESH,
        )

    def link_sems(i, p):
        return b_send.at[i, p], b_recv.at[i, p]

    def block_slot(i, p):
        dy, dx = plane[p]
        return slot_of(sender(y, Y, dy), core, sender(z, Z, i), sender(x, X, dx))

    started = []
    def start(copy):
        copy.start()
        started.append(copy)
        return copy

    def to_plane(i, src):
        return [
            start(send(src, block_slot(i, 0), link_sems(i, p), p_peers[p]))
            for p in range(len(plane) - 1, 0, -1)
        ][::-1]

    def to_twin(i, p, src):
        return start(send(src, block_slot(i, p), (c_send.at[i, p], c_recv.at[i, p]), twin))

    arrivals = {}
    load_own.wait()
    emb = slots.at[mine]
    for i in range(Z - 1, 0, -1):
        arrivals[i, 0] = start(send(emb, mine, link_sems(i, 0), z_peers[i]))
    for p, copy in enumerate(to_plane(0, emb)):
        arrivals[0, p + 1] = copy
    over = [to_twin(0, 0, emb)]
    load.start()
    for i in range(1, Z):
        arrivals[i, 0].wait_recv()
        src = slots.at[block_slot(i, 0)]
        for p, copy in enumerate(to_plane(i, src)):
            arrivals[i, p + 1] = copy
        over.append(to_twin(i, 0, src))
    for i in range(Z):
        for p in range(1, len(plane)):
            arrivals[i, p].wait_recv()
            over.append(to_twin(i, p, slots.at[block_slot(i, p)]))
    step = min(8, devices // 2)

    def lay_out(first):
        @pl.loop(0, devices // 2 // step)
        def _(i):
            part = slots[pl.ds(first + i * step, step)].astype(jnp.float32)
            rows = pl.ds(pl.multiple_of((first + i * step) * local, step * local), step * local)
            gathered[rows, :] = part.reshape(step * local, part.shape[2]).astype(jnp.bfloat16)

    lay_out(core * (devices // 2))
    load.wait()
    for copy in over:
        copy.wait_recv()
    lay_out((1 - core) * (devices // 2))
    tile = 256
    wide = min(n, 256)
    me = r * cents + c

    @pl.loop(0, n // wide)
    def _(j):
        lanes = pl.ds(pl.multiple_of(j * wide, wide), wide)
        top = jnp.full((8, wide), -jnp.inf, jnp.float32)
        for t in range(k // tile):
            rows = pl.ds(t * tile, tile)
            part = inverse_temp * lax.dot_general(
                cen_v[rows, :], gathered[lanes, :], NT, preferred_element_type=jnp.float32
            )
            shifted[rows, lanes] = part
            top = jnp.maximum(top, jnp.max(part.reshape(tile // 8, 8, wide), axis=0))
        top = jnp.max(top, axis=0, keepdims=True)
        total = jnp.zeros((8, wide), jnp.float32)
        for t in range(k // tile):
            rows = pl.ds(t * tile, tile)
            part = jnp.exp(shifted[rows, lanes] - top)
            shifted[rows, lanes] = part
            total = total + jnp.sum(part.reshape(tile // 8, 8, wide), axis=0)
        tops[:, lanes] = top
        stats[me, :, lanes] = top + jnp.log(jnp.sum(total, axis=0, keepdims=True))

    offsets = [
        (i, j, l, m) for m in range(2) for i in range(Y) for j in range(X) for l in range(Z)
    ]
    for i, j, l, m in reversed(offsets[1:]):
        peer = place(flipped(y, Y, i), (core + m) % 2, flipped(z, Z, l), flipped(x, X, j))
        pltpu.make_async_remote_copy(
            src_ref=stats.at[me], dst_ref=stats.at[me], send_sem=s_send, recv_sem=s_recv,
            device_id=peer, device_id_type=MESH,
        ).start()
    for copy in started:
        copy.wait_send()

    others = stats.at[pl.ds(0, devices - 1)]
    pltpu.make_async_copy(others, others, s_recv).wait()

    @pl.loop(0, n // wide)
    def _(j):
        lanes = pl.ds(pl.multiple_of(j * wide, wide), wide)
        part_lse = stats[:, :, lanes]
        top = jnp.max(part_lse, axis=0)
        lse = top + jnp.log(jnp.sum(jnp.exp(part_lse - top[None]), axis=0))
        lse_out[:, lanes] = lse
        factor = jnp.exp(tops[:, lanes] - lse)
        for t in range(k // tile):
            rows = pl.ds(t * tile, tile)
            resp[rows, lanes] = (shifted[rows, lanes] * factor).astype(jnp.bfloat16)

    pltpu.make_async_copy(others, others, s_send).wait()


def sums_kernel(
    sizes, lse, resp, gathered, lse_out, counts_out, sums_out,
    lse_v, counts_v, sums_v, lse_sem, counts_sem, out_sem,
):
    Y, X, Z = sizes
    n = gathered.shape[0]
    k = resp.shape[0]
    local = lse_out.shape[1]
    r = lax.axis_index("rows")
    c = lax.axis_index("cent")
    slot = (((r % 2) * Y + r // 2) * X + c % X) * Z + c // X

    outs = []
    for t in range(k // SUMS_TILE):
        rows = pl.ds(t * SUMS_TILE, SUMS_TILE)
        sums_v[rows, :] = lax.dot_general(
            resp[rows, :], gathered[...], NN, preferred_element_type=jnp.float32
        ).astype(jnp.bfloat16)
        outs.append(pltpu.make_async_copy(sums_v.at[rows], sums_out.at[rows], out_sem.at[t]))
        outs[-1].start()
        if t == 1:
            rolled = pltpu.roll(jnp.broadcast_to(lse[...], (8, n)), n - slot * local, 1)
            lse_v[...] = rolled[0:1, :local]
            outs.append(pltpu.make_async_copy(lse_v, lse_out, lse_sem))
            outs[-1].start()
            counts_v[...] = lax.dot_general(
                jnp.ones((8, n), jnp.bfloat16), resp[...], NT,
                preferred_element_type=jnp.float32,
            )[0:1]
            outs.append(pltpu.make_async_copy(counts_v, counts_out, counts_sem))
            outs[-1].start()
    for copy in outs:
        copy.wait()


def on_device(sizes, embeddings, centroids):
    Y, X, Z = sizes
    devices = 2 * Y * X * Z
    local, depth = embeddings.shape
    k = centroids.shape[0]
    n = local * devices
    dma = pltpu.SemaphoreType.DMA
    vmem = pl.BlockSpec(memory_space=pltpu.VMEM)
    hbm = pl.BlockSpec(memory_space=pltpu.HBM)
    embeddings = pltpu.with_memory_space_constraint(embeddings, pltpu.HBM)
    centroids = pltpu.with_memory_space_constraint(centroids, pltpu.HBM)
    lse, resp, gathered = pl.pallas_call(
        functools.partial(spread_kernel, sizes),
        out_shape=(
            jax.ShapeDtypeStruct((1, n), jnp.float32),
            jax.ShapeDtypeStruct((k, n), jnp.bfloat16),
            jax.ShapeDtypeStruct((n, depth), jnp.bfloat16),
        ),
        in_specs=[hbm, hbm],
        out_specs=(vmem, vmem, vmem),
        scratch_shapes=[
            pltpu.VMEM((k, depth), jnp.bfloat16),
            pltpu.VMEM((devices, local, depth), jnp.bfloat16),
            pltpu.VMEM((k, n), jnp.float32),
            pltpu.VMEM((1, n), jnp.float32),
            pltpu.VMEM((devices, 1, n), jnp.float32),
            dma, dma,
            dma((Z, Y * X)), dma((Z, Y * X)),
            dma((Z, Y * X)), dma((Z, Y * X)),
            dma, dma,
        ],
        compiler_params=pltpu.CompilerParams(
            collective_id=0, has_side_effects=True, vmem_limit_bytes=32 * 2**20
        ),
    )(embeddings, centroids)
    own_lse, counts, sums = pl.pallas_call(
        functools.partial(sums_kernel, sizes),
        out_shape=(
            jax.ShapeDtypeStruct((1, local), jnp.float32),
            jax.ShapeDtypeStruct((1, k), jnp.float32),
            jax.ShapeDtypeStruct((k, depth), jnp.bfloat16),
        ),
        in_specs=[vmem, vmem, vmem],
        out_specs=(hbm, hbm, hbm),
        scratch_shapes=[
            pltpu.VMEM((1, local), jnp.float32),
            pltpu.VMEM((1, k), jnp.float32),
            pltpu.VMEM((k, depth), jnp.bfloat16),
            dma, dma,
            dma((k // SUMS_TILE,)),
        ],
        compiler_params=pltpu.CompilerParams(vmem_limit_bytes=16 * 2**20),
    )(lse, resp, gathered)
    return own_lse.reshape(local), sums, counts.reshape(k)


def solution(mesh):
    rows, cents = mesh.shape["rows"], mesh.shape["cent"]
    Y = rows // 2
    X = Y if cents % Y == 0 else 1
    return jax.shard_map(
        functools.partial(on_device, (Y, X, cents // X)),
        mesh=mesh,
        in_specs=(P(("rows", "cent"), None), P(("rows", "cent"), None)),
        out_specs=(P(("rows", "cent")), P(("rows", "cent"), None), P(("rows", "cent"))),
        check_vma=False,
    )
```
